256 devices in a mesh: row: 16 (over x_hi, z), col: 8 (over x_lo, y), cores: 2 (over core).
Axes of the slice: x: 4 (x_hi: 2, x_lo: 2; x = x_hi * 2 + x_lo), y: 4, z: 8, core: 2. Of those that a mesh axis runs over, the one named last changes fastest.
Arguments:
- batch_index: int32 [32768], P(('row', 'col')), may hold values from 0 to 511, as said below
- chip_features: bfloat16 [65536, 2048], P(('row', 'col')), may hold values from -6 to 6
- head_weight: bfloat16 [2048, 128], replicated, may hold values from -0.125 to 0.125
- probe_left: bfloat16 [32768, 64], P(('row', 'col'), 'cores'), may hold values from -2.5 to 2.5
- probe_right: bfloat16 [32768, 64], P(('row', 'col'), 'cores'), may hold values from -2.5 to 2.5
Outputs:
- embed_grad: float32 [32768, 128], P(('row', 'col'))
- head_grad: float32 [2048, 128], replicated
The draws below stay inside these ranges and needn't reach their ends.
Inputs may be any that keep to these rules, and one draw needn't show every extreme that they name: `batch_index`: within each aligned block of 256 points the indices are distinct; they count the chips held with that block, from its first one.
All inputs are finite; a program needn't handle non-finite values.
Results may differ from the reference program's by a relative error of at most 0.0041.
Values may be sent and summed in bfloat16 or wider, within the bound.
A program may use at most 64 MiB of HBM per device.

```python
import math
import jax
import jax.numpy as jnp
from jax import lax

E = 128
H = 2048
PROBES = 64
PTS_DEV = 256
TOKENS = 32768
CHIPS_DEV = 512
CHIPS = 65536


def draw_batch_index(key, part):
    key = jax.random.fold_in(key, 11)
    block_count = TOKENS // PTS_DEV
    block_keys = jax.random.split(key, block_count)

    def one_block(block_key):
        first_key, second_key = jax.random.split(block_key)
        middle = (jax.random.permutation(first_key, CHIPS_DEV - 2) + 1).astype(jnp.int32)
        chosen = jnp.concatenate([jnp.zeros((1,), jnp.int32), middle[:PTS_DEV - 2], jnp.full((1,), CHIPS_DEV - 1, jnp.int32)])
        return jax.random.permutation(second_key, chosen)
    return jax.vmap(one_block)(block_keys).reshape(TOKENS).astype(jnp.int32)


def block_levels(stream_key, extent, pieces, low, top_value):
    gain = 1.0
    for position, blocks in pieces:
        heights = jax.random.uniform(jax.random.fold_in(jax.random.fold_in(stream_key, 6), position), (blocks,), jnp.float32, low / len(pieces), top_value / len(pieces))
        gain = gain * jnp.repeat(jnp.exp(heights), extent[position] // blocks).reshape((-1,) + (1,) * (len(extent) - 1 - position))
    return gain


def noise(key, shape, spread, bound, shards=(), held_as=jnp.bfloat16):
    values = spread * jax.random.normal(key, shape, jnp.float32)
    if shards:
        values = values * block_levels(key, shape, shards, -0.22, 0.18)
    return jnp.clip(values, -bound, bound).astype(held_as)


def setup_inputs(seed: int = 0) -> dict:
    key_list = jax.random.split(jax.random.key(seed), 6)
    return {
        "batch_index": draw_batch_index(jax.random.fold_in(key_list[5], 71), 0),
        "chip_features": noise(key_list[1], (CHIPS, H), 1.0, 6.0, ((0, 128),)),
        "head_weight": noise(key_list[2], (H, E), H ** -0.5, 0.125),
        "probe_left": noise(key_list[3], (TOKENS, PROBES), 0.35, 2.5, ((0, 128), (1, 2))),
        "probe_right": noise(key_list[4], (TOKENS, PROBES), 0.35, 2.5, ((0, 128), (1, 2))),
    }


def reference(batch_index, chip_features, head_weight, probe_left, probe_right):
    device_block = jnp.arange(TOKENS, dtype=jnp.int32) // PTS_DEV
    global_index = (batch_index + device_block * CHIPS_DEV).astype(jnp.int32)
    features = jnp.take(chip_features, global_index, axis=0)
    embedding = jnp.dot(features, head_weight, preferred_element_type=jnp.float32).astype(jnp.bfloat16)
    embed_float = embedding.astype(jnp.float32)
    squares = lax.optimization_barrier(jnp.sum(embed_float * embed_float, axis=1))
    per_core = PROBES // 2
    block_rows = min(2048, TOKENS)
    block_count = TOKENS // block_rows
    exponent_scale = 0.5 / E
    inverse_width = 1.0 / E

    def advance(column_total, block_id):
        offset = (block_id * block_rows).astype(jnp.int32)
        rows_embed = lax.dynamic_slice_in_dim(embedding, offset, block_rows, 0)
        rows_float = rows_embed.astype(jnp.float32)
        rows_square = lax.dynamic_slice_in_dim(squares, offset, block_rows, 0)
        rows_left = lax.dynamic_slice_in_dim(probe_left, offset, block_rows, 0)
        products = lax.dot_general(rows_embed, embedding, (((1,), (1,)), ((), ())), preferred_element_type=jnp.float32)
        kernel_tile = jnp.exp(-(rows_square[:, None] + squares[None, :] - 2.0 * products) * exponent_scale)
        row_part = jnp.zeros((block_rows, E), jnp.float32)
        for which in range(2):
            left_set = rows_left[:, which * per_core:(which + 1) * per_core]
            right_set = probe_right[:, which * per_core:(which + 1) * per_core]
            intersection = lax.dot_general(left_set, right_set, (((1,), (1,)), ((), ())), preferred_element_type=jnp.float32)
            weight_tile = kernel_tile * intersection * inverse_width
            rounded_tile = weight_tile.astype(jnp.bfloat16)
            row_part = row_part + jnp.dot(rounded_tile, embedding, preferred_element_type=jnp.float32) - lax.optimization_barrier(jnp.sum(weight_tile, axis=1))[:, None] * rows_float
            column_total = column_total + lax.dot_general(rounded_tile, rows_embed, (((0,), (0,)), ((), ())), preferred_element_type=jnp.float32) - lax.optimization_barrier(jnp.sum(weight_tile, axis=0))[:, None] * embed_float
        return (column_total, row_part)
    column_total, row_parts = lax.scan(advance, jnp.zeros((TOKENS, E), jnp.float32), jnp.arange(block_count, dtype=jnp.int32))
    embed_grad = row_parts.reshape(TOKENS, E) + column_total
    head_grad = jnp.dot(features.astype(jnp.float32).T, embed_grad, precision=lax.Precision.HIGHEST) * (1.0 / math.sqrt(TOKENS))
    return (embed_grad, head_grad)
```

```python
import functools
import math

import jax
import jax.numpy as jnp
from jax import lax
from jax.experimental import pallas as pl
from jax.experimental.pallas import tpu as pltpu
from jax.sharding import PartitionSpec as P

MESH = pl.DeviceIdType.MESH
F32, BF16 = jnp.float32, jnp.bfloat16
NX, NY, NZ = 4, 4, 8
PLANE = NX * NY


def dot(a, b, ca, cb):
    return lax.dot_general(a, b, (((ca,), (cb,)), ((), ())), preferred_element_type=F32)


def squares(z):
    zf = z.astype(F32)
    sq = zf * zf
    hi = sq.astype(BF16)
    return hi, (sq - hi.astype(F32)).astype(BF16)


def fused(norm, idx_ref, feat_hbm, w_hbm, left_ref, right_ref, head_out, embed_out,
          feat, w, e_all, ft, u_buf, u_in, z_own, zA, lrA, qA, zB, rlB, qB, acc, mass,
          gs, gr, gfull, hp, hr, hz, hb,
          feat_sem, w_sem, u_sem, az_s, az_r, al_s, al_r, fz_s, fz_r, fl_s, fl_r,
          bz_s, bz_r, bl_s, bl_r, g_s, g_r, gx_sem, hr_s, hr_r, hz_s, hz_r, ha_s, ha_r, hf_s, hf_r):
    row, col, core = lax.axis_index("row"), lax.axis_index("col"), lax.axis_index("cores")
    x, y, z = (row // NZ) * 2 + col // NY, col % NY, row % NZ
    half = z_own.shape[1]
    embed = z_own.shape[2]
    scale = 0.5 / embed * math.log2(math.e)

    def at(dx, dy, dz, dc):
        nx, ny, nz = (x + dx) % NX, (y + dy) % NY, (z + dz) % NZ
        return ((nx // 2) * NZ + nz, (nx % 2) * NY + ny, (core + dc) % 2)

    def plane_at(n):
        return at(n // NY, n % NY, 0, 0)

    def remote(src, dst, ssem, rsem, device):
        return pltpu.make_async_remote_copy(
            src_ref=src, dst_ref=dst, send_sem=ssem, recv_sem=rsem, device_id=device, device_id_type=MESH)

    sibling = at(0, 0, 0, 1)
    me_plane = x * NY + y
    other = 1 - core

    chunk = feat.shape[0] // 4
    w_copy = pltpu.make_async_copy(w_hbm, w, w_sem)
    w_copy.start()
    feat_copies = [
        pltpu.make_async_copy(feat_hbm.at[pl.ds(i * chunk, chunk)], feat.at[pl.ds(i * chunk, chunk)], feat_sem.at[i])
        for i in range(4)]
    for c in feat_copies:
        c.start()

    barrier = pltpu.get_barrier_semaphore()
    for n in range(1, PLANE):
        pl.semaphore_signal(barrier, inc=1, device_id=plane_at(n), device_id_type=MESH)
    for j in range(1, NZ):
        pl.semaphore_signal(barrier, inc=1, device_id=at(0, 0, j, 0), device_id_type=MESH)
    pl.semaphore_signal(barrier, inc=1, device_id=sibling, device_id_type=MESH)

    probes = left_ref.shape[1]
    lane = lax.broadcasted_iota(jnp.int32, (probes, embed), 1)
    sub = lax.broadcasted_iota(jnp.int32, (probes, embed), 0)
    first = (lane == sub + 2 * probes * core).astype(F32).astype(BF16)
    second = (lane == sub + 2 * probes * core + probes).astype(F32).astype(BF16)
    lv, rv = left_ref[...], right_ref[...]
    u = (dot(lv, first, 1, 0) + dot(rv, second, 1, 0)).astype(BF16)
    v = (dot(lv, second, 1, 0) + dot(rv, first, 1, 0)).astype(BF16)
    for h in range(2):
        u_buf[h, 0] = u[h * half:(h + 1) * half]
        u_buf[h, 1] = v[h * half:(h + 1) * half]

    w_copy.wait()
    for i, c in enumerate(feat_copies):
        c.wait()
        e_all[pl.ds(i * chunk, chunk)] = dot(feat[pl.ds(i * chunk, chunk)], w[...], 1, 0).astype(BF16)
    index = idx_ref[...].reshape(1, 2 * half)
    onehot = (lax.broadcasted_iota(jnp.int32, (feat.shape[0], 2 * half), 0) == index).astype(F32).astype(BF16)
    z_all = dot(onehot, e_all[...], 0, 0).astype(BF16)
    z_own[0] = z_all[:half]
    z_own[1] = z_all[half:]
    mine = z_own[core]
    zA[0, 0] = mine
    zA[1, 0] = z_own[other]
    zB[0] = mine

    pl.semaphore_wait(barrier, PLANE - 1 + NZ - 1 + 1)

    u_copy = remote(u_buf.at[other], u_in, u_sem.at[0], u_sem.at[1], sibling)
    u_copy.start()
    za_copies = [None] + [remote(zA.at[0, 0], zA.at[0, n], az_s.at[n], az_r.at[n], plane_at(n)) for n in range(1, PLANE)]
    zb_copies = [None] + [remote(zB.at[0], zB.at[j], bz_s.at[j], bz_r.at[j], at(0, 0, j, 0)) for j in range(1, NZ)]
    for n in range(1, PLANE):
        za_copies[n].start()
        if n < NZ:
            zb_copies[n].start()
    u_copy.wait_recv()
    lrA[0, 0] = u_buf[core, 0] + u_in[0]
    rlB[0] = u_buf[core, 1] + u_in[1]
    la_copies = [None] + [remote(lrA.at[0, 0], lrA.at[0, n], al_s.at[n], al_r.at[n], plane_at(n)) for n in range(1, PLANE)]
    lb_copies = [None] + [remote(rlB.at[0], rlB.at[j], bl_s.at[j], bl_r.at[j], at(0, 0, j, 0)) for j in range(1, NZ)]
    for n in range(1, PLANE):
        la_copies[n].start()
        if n < NZ:
            lb_copies[n].start()
    fl_copies = [remote(lrA.at[0, n], lrA.at[1, n], fl_s.at[n], fl_r.at[n], sibling) for n in range(PLANE)]
    fz_copies = [None] + [remote(zA.at[0, n], zA.at[1, n], fz_s.at[n], fz_r.at[n], sibling) for n in range(1, PLANE)]
    fl_copies[0].start()

    columns = feat.shape[1] // 2
    ft[...] = dot(feat[:, pl.ds(pl.multiple_of(core * columns, columns), columns)], onehot, 0, 0).astype(BF16)
    acc[...] = jnp.zeros_like(acc)
    mass[...] = jnp.zeros_like(mass)
    ones = jnp.ones((8, embed), BF16)

    def norms_a(h, n):
        hi, lo = squares(zA[h, n])
        qA[h, n] = (dot(ones, hi, 1, 1) + dot(ones, lo, 1, 1)) * scale

    def norms_b(j):
        hi, lo = squares(zB[j])
        wide = jnp.ones((embed, embed), BF16)
        qB[j] = (dot(hi, wide, 1, 0) + dot(lo, wide, 1, 0)) * scale

    norms_a(0, 0)
    norms_a(1, 0)
    norms_b(0)
    for n in range(1, PLANE):
        za_copies[n].wait_recv()
        fz_copies[n].start()
        norms_a(0, n)
        if n < NZ:
            zb_copies[n].wait_recv()
            norms_b(n)
    for j in range(1, NZ):
        lb_copies[j].wait_recv()

    def tile(h, m, j, blocks):
        rows = blocks * half
        zb = zB[pl.ds(j, blocks)].reshape(rows, embed)
        rl = rlB[pl.ds(j, blocks)].reshape(rows, embed)
        qb = qB[pl.ds(j, blocks)].reshape(rows, embed)
        za = zA[h, pl.ds(2 * m, 2)].reshape(2 * half, embed)
        lr = lrA[h, pl.ds(2 * m, 2)].reshape(2 * half, embed)
        qa = jnp.concatenate([qA[h, 2 * m, 0:1], qA[h, 2 * m + 1, 0:1]], axis=1)
        products = dot(zb, za, 1, 1)
        pairs = dot(rl, lr, 1, 1)
        weight = jnp.exp2(products * (2.0 * scale) - (jnp.concatenate([qb, qb], axis=1) + qa)) * pairs
        part = dot(weight.astype(BF16), za, 1, 0)
        acc[pl.ds(j, blocks)] += part.reshape(blocks, half, embed)
        mass[pl.ds(j, blocks)] += (weight[:, :half] + weight[:, half:]).reshape(blocks, half, embed)

    def first_half(m, carry):
        for n in (2 * m, 2 * m + 1):
            @pl.when(n > 0)
            def _():
                remote(lrA.at[0, 0], lrA.at[0, n], al_s.at[n], al_r.at[n], sibling).wait_recv()
                remote(lrA.at[0, n], lrA.at[1, n], fl_s.at[n], fl_r.at[n], sibling).start()
        for j in range(0, NZ, 2):
            tile(0, m, j, 2)
        return carry

    lax.fori_loop(0, PLANE // 2, first_half, 0)

    for n in range(1, PLANE):
        fz_copies[n].wait_recv()
        norms_a(1, n)
    for n in range(PLANE):
        fl_copies[n].wait_recv()

    g_copies = [None] + [remote(gs.at[j], gr.at[j], g_s.at[j], g_r.at[j], at(0, 0, NZ - j, 0)) for j in range(1, NZ)]
    for j in (4, 2, 6, 0):
        def second_half(m, carry, j=j):
            tile(1, m, j, 2)
            return carry

        lax.fori_loop(0, PLANE // 2, second_half, 0)
        for i in (j, j + 1):
            total = jnp.sum(mass[i], axis=1, keepdims=True)
            grad = (acc[i] - total * zB[i].astype(F32)) * (1.0 / embed)
            if i == 0:
                acc[0] = grad
            else:
                gs[i] = grad.astype(BF16)
                g_copies[i].start()

    for n in range(1, PLANE):
        za_copies[n].wait_send()
        la_copies[n].wait_send()
        fz_copies[n].wait_send()
    for n in range(PLANE):
        fl_copies[n].wait_send()
    for j in range(1, NZ):
        zb_copies[j].wait_send()
        lb_copies[j].wait_send()
    u_copy.wait_send()

    grad = acc[0]
    for j in range(1, NZ):
        g_copies[j].wait_recv()
        grad = grad + gr[j].astype(F32)
    gfull[core] = grad
    gx = remote(gfull.at[core], gfull.at[core], gx_sem.at[0], gx_sem.at[1], sibling)
    gx.start()
    for j in range(1, NZ):
        g_copies[j].wait_send()
    gx.wait()

    both = gfull[...].reshape(2 * half, embed)
    embed_out[...] = both
    hi = both.astype(BF16)
    lo = (both - hi.astype(F32)).astype(BF16)
    wide = dot(ft[...], jnp.concatenate([hi, lo], axis=1), 1, 0)
    hp[...] = (wide[:, :embed] + wide[:, embed:]).astype(BF16).reshape(hp.shape)

    def slice_of(n):
        return ((x + n // NY) % NX) * NY + (y + n % NY) % NY

    hr_copies = [None] + [remote(hp.at[slice_of(n)], hr.at[n], hr_s.at[n], hr_r.at[n], plane_at(n)) for n in range(1, PLANE)]
    for n in range(1, PLANE):
        hr_copies[n].start()
    total = hp[me_plane].astype(F32)
    for n in range(1, PLANE):
        hr_copies[n].wait_recv()
        total = total + hr[n].astype(F32)
    hz[z] = (total * norm).astype(BF16)

    hz_copies = [None] + [remote(hz.at[z], hz.at[z], hz_s.at[j], hz_r.at[j], at(0, 0, j, 0)) for j in range(1, NZ)]
    for j in range(1, NZ):
        hz_copies[j].start()
    for n in range(1, PLANE):
        hr_copies[n].wait_send()
    for j in range(1, NZ):
        hz_copies[j].wait_recv()
    total = hz[0].astype(F32)
    for j in range(1, NZ):
        total = total + hz[j].astype(F32)
    hb[core, me_plane] = total.astype(BF16)

    ha_copies = [None] + [
        remote(hb.at[core, me_plane], hb.at[core, me_plane], ha_s.at[n], ha_r.at[n], plane_at(n)) for n in range(1, PLANE)]
    for n in range(1, PLANE):
        ha_copies[n].start()
    hf_copies = []
    for n in range(PLANE):
        source = ((x + NX - n // NY) % NX) * NY + (y + NY - n % NY) % NY
        if n:
            ha_copies[n].wait_recv()
        c = remote(hb.at[core, source], hb.at[core, source], hf_s.at[n], hf_r.at[n], sibling)
        c.start()
        hf_copies.append(c)
    for j in range(1, NZ):
        hz_copies[j].wait_send()
    for n in range(1, PLANE):
        ha_copies[n].wait_send()
    for c in hf_copies:
        c.wait()
    head_out[...] = hb[...].reshape(head_out.shape)


def finish(head_in, embed_in, embed_out, head_out):
    embed_out[...] = embed_in[...]
    head_out[...] = head_in[...].astype(F32)


def local(batch_index, chip_features, head_weight, probe_left, probe_right):
    points = batch_index.shape[0]
    half = points // 2
    chips, width = chip_features.shape
    embed = head_weight.shape[1]
    rows = width // 2 // PLANE
    norm = 1.0 / math.sqrt(points * PLANE * NZ)
    block = (half, embed)
    vmem, dma = pltpu.VMEM, pltpu.SemaphoreType.DMA
    head, grad = pl.pallas_call(
        functools.partial(fused, norm),
        out_shape=(jax.ShapeDtypeStruct((width, embed), BF16), jax.ShapeDtypeStruct((points, embed), F32)),
        in_specs=[pl.BlockSpec(memory_space=pltpu.VMEM), pl.BlockSpec(memory_space=pl.ANY),
                  pl.BlockSpec(memory_space=pl.ANY), pl.BlockSpec(memory_space=pltpu.VMEM),
                  pl.BlockSpec(memory_space=pltpu.VMEM)],
        out_specs=[pl.BlockSpec(memory_space=pltpu.VMEM)] * 2,
        scratch_shapes=[
            vmem((chips, width), BF16), vmem((width, embed), BF16), vmem((chips, embed), BF16),
            vmem((width // 2, points), BF16), vmem((2, 2) + block, BF16), vmem((2,) + block, BF16),
            vmem((2,) + block, BF16), vmem((2, PLANE) + block, BF16), vmem((2, PLANE) + block, BF16),
            vmem((2, PLANE, 8, half), F32), vmem((NZ,) + block, BF16), vmem((NZ,) + block, BF16),
            vmem((NZ,) + block, F32), vmem((NZ,) + block, F32), vmem((NZ,) + block, F32),
            vmem((NZ,) + block, BF16), vmem((NZ,) + block, BF16), vmem((2,) + block, F32),
            vmem((PLANE, rows, embed), BF16), vmem((PLANE, rows, embed), BF16),
            vmem((NZ, rows, embed), BF16), vmem((2, PLANE, rows, embed), BF16),
            dma((4,)), dma, dma((2,)),
            dma((PLANE,)), dma((PLANE,)), dma((PLANE,)), dma((PLANE,)),
            dma((PLANE,)), dma((PLANE,)), dma((PLANE,)), dma((PLANE,)),
            dma((NZ,)), dma((NZ,)), dma((NZ,)), dma((NZ,)), dma((NZ,)), dma((NZ,)), dma((2,)),
            dma((PLANE,)), dma((PLANE,)), dma((NZ,)), dma((NZ,)),
            dma((PLANE,)), dma((PLANE,)), dma((PLANE,)), dma((PLANE,)),
        ],
        compiler_params=pltpu.CompilerParams(
            collective_id=0, has_side_effects=True, vmem_limit_bytes=48 * 2**20),
    )(batch_index, chip_features, head_weight, probe_left, probe_right)
    return pl.pallas_call(
        finish,
        out_shape=(jax.ShapeDtypeStruct((points, embed), F32), jax.ShapeDtypeStruct((width, embed), F32)),
        in_specs=[pl.BlockSpec(memory_space=pltpu.VMEM)] * 2,
        out_specs=[pl.BlockSpec(memory_space=pltpu.VMEM)] * 2,
    )(head, grad)


def solution(mesh):
    return jax.shard_map(
        local,
        mesh=mesh,
        in_specs=(P(("row", "col")), P(("row", "col"), None), P(), P(("row", "col"), "cores"), P(("row", "col"), "cores")),
        out_specs=(P(("row", "col"), None), P()),
        check_vma=False,
    )
```

```python
import functools
import math

import jax
import jax.numpy as jnp
from jax import lax
from jax.experimental import pallas as pl
from jax.experimental.pallas import tpu as pltpu
from jax.sharding import PartitionSpec as P

MESH = pl.DeviceIdType.MESH
F32, BF16 = jnp.float32, jnp.bfloat16
NX, NY, NZ = 4, 4, 8
PLANE = NX * NY


def dot(a, b, ca, cb):
    return lax.dot_general(a, b, (((ca,), (cb,)), ((), ())), preferred_element_type=F32)


def squares(z):
    zf = z.astype(F32)
    sq = zf * zf
    hi = sq.astype(BF16)
    return hi, (sq - hi.astype(F32)).astype(BF16)


def fused(norm, idx_hbm, feat_hbm, w_hbm, left_hbm, right_hbm, head_out, embed_out,
          idx_ref, left_ref, right_ref, feat, w, e_all, ft, u_buf, u_in, z_own, zA, lrA, qA, zB, rlB, qB, acc, mass,
          gs, gr, gfull, hp, hr, hz, hb,
          feat_sem, in_sem, u_sem, az_s, az_r, al_s, al_r, fz_s, fz_r, fl_s, fl_r,
          bz_s, bz_r, bl_s, bl_r, g_s, g_r, gx_sem, hr_s, hr_r, hz_s, hz_r, ha_s, ha_r, hf_s, hf_r):
    row, col, core = lax.axis_index("row"), lax.axis_index("col"), lax.axis_index("cores")
    x, y, z = (row // NZ) * 2 + col // NY, col % NY, row % NZ
    half = z_own.shape[1]
    embed = z_own.shape[2]
    scale = 0.5 / embed * math.log2(math.e)

    def at(dx, dy, dz, dc):
        nx, ny, nz = (x + dx) % NX, (y + dy) % NY, (z + dz) % NZ
        return ((nx // 2) * NZ + nz, (nx % 2) * NY + ny, (core + dc) % 2)

    def plane_at(n):
        return at(n // NY, n % NY, 0, 0)

    def remote(src, dst, ssem, rsem, device):
        return pltpu.make_async_remote_copy(
            src_ref=src, dst_ref=dst, send_sem=ssem, recv_sem=rsem, device_id=device, device_id_type=MESH)

    sibling = at(0, 0, 0, 1)
    me_plane = x * NY + y
    other = 1 - core

    chunk = feat.shape[0] // 4
    small_copies = [
        pltpu.make_async_copy(src, dst, in_sem.at[i])
        for i, (src, dst) in enumerate(((left_hbm, left_ref), (right_hbm, right_ref), (idx_hbm, idx_ref), (w_hbm, w)))]
    for c in small_copies:
        c.start()
    feat_copies = [
        pltpu.make_async_copy(feat_hbm.at[pl.ds(i * chunk, chunk)], feat.at[pl.ds(i * chunk, chunk)], feat_sem.at[i])
        for i in range(4)]
    for c in feat_copies:
        c.start()

    barrier = pltpu.get_barrier_semaphore()
    for n in range(1, PLANE):
        pl.semaphore_signal(barrier, inc=1, device_id=plane_at(n), device_id_type=MESH)
    for j in range(1, NZ):
        pl.semaphore_signal(barrier, inc=1, device_id=at(0, 0, j, 0), device_id_type=MESH)
    pl.semaphore_signal(barrier, inc=1, device_id=sibling, device_id_type=MESH)

    probes = left_ref.shape[0]
    lane = lax.broadcasted_iota(jnp.int32, (probes, embed), 1)
    sub = lax.broadcasted_iota(jnp.int32, (probes, embed), 0)
    first = (lane == sub + 2 * probes * core).astype(F32).astype(BF16)
    second = (lane == sub + 2 * probes * core + probes).astype(F32).astype(BF16)
    small_copies[0].wait()
    small_copies[1].wait()
    lv, rv = left_ref[...], right_ref[...]
    u = (dot(lv, first, 0, 0) + dot(rv, second, 0, 0)).astype(BF16)
    v = (dot(lv, second, 0, 0) + dot(rv, first, 0, 0)).astype(BF16)
    for h in range(2):
        u_buf[h, 0] = u[h * half:(h + 1) * half]
        u_buf[h, 1] = v[h * half:(h + 1) * half]

    small_copies[3].wait()
    for i, c in enumerate(feat_copies):
        c.wait()
        e_all[pl.ds(i * chunk, chunk)] = dot(feat[pl.ds(i * chunk, chunk)], w[...], 1, 0).astype(BF16)
    small_copies[2].wait()
    index = idx_ref[...].reshape(1, 2 * half)
    onehot = (lax.broadcasted_iota(jnp.int32, (feat.shape[0], 2 * half), 0) == index).astype(F32).astype(BF16)
    z_all = dot(onehot, e_all[...], 0, 0).astype(BF16)
    z_own[0] = z_all[:half]
    z_own[1] = z_all[half:]
    mine = z_own[core]
    zA[0, 0] = mine
    zA[1, 0] = z_own[other]
    zB[0] = mine

    pl.semaphore_wait(barrier, PLANE - 1 + NZ - 1 + 1)

    sends = []

    def send(src, dst, ssem, rsem, device):
        c = remote(src, dst, ssem, rsem, device)
        c.start()
        sends.append(c)
        return c

    def send_z(n, m):
        d = m - n
        return send(zA.at[0, n], zA.at[0, m], az_s.at[m], az_r.at[m], plane_at(d))

    def send_l(n, m):
        return send(lrA.at[0, n], lrA.at[0, m], al_s.at[m], al_r.at[m], plane_at(m - n))

    def line_z(i, j):
        return send(zB.at[i], zB.at[j], bz_s.at[j], bz_r.at[j], at(0, 0, (j - i) % NZ, 0))

    def line_l(i, j):
        return send(rlB.at[i], rlB.at[j], bl_s.at[j], bl_r.at[j], at(0, 0, (j - i) % NZ, 0))

    def arrived(buf, sems):
        remote(buf, buf, sems, sems, sibling).wait_recv()

    u_copy = send(u_buf.at[other], u_in, u_sem.at[0], u_sem.at[1], sibling)
    near = (1, 3, 2)
    for d in near:
        send_z(0, NY * d)
    line_z(0, 2)
    line_z(0, 6)
    for d in near:
        send_z(0, d)
    line_z(0, 1)
    line_z(0, 7)
    u_copy.wait_recv()
    lrA[0, 0] = u_buf[core, 0] + u_in[0]
    rlB[0] = u_buf[core, 1] + u_in[1]
    for d in near:
        send_l(0, d)
    line_l(0, 2)
    line_l(0, 6)
    for d in near:
        send_l(0, NY * d)
    line_l(0, 1)
    line_l(0, 7)

    def forward_z(n):
        return remote(zA.at[0, n], zA.at[1, n], fz_s.at[n], fz_r.at[n], sibling)

    def forward_l(n):
        return remote(lrA.at[0, n], lrA.at[1, n], fl_s.at[n], fl_r.at[n], sibling)

    forward_l(0).start()
    ones = jnp.ones((8, embed), BF16)

    def norms_a(h, n):
        hi, lo = squares(zA[h, n])
        qA[h, n] = (dot(ones, hi, 1, 1) + dot(ones, lo, 1, 1)) * scale

    def norms_b(j):
        hi, lo = squares(zB[j])
        wide = jnp.ones((embed, embed), BF16)
        qB[j] = (dot(hi, wide, 1, 0) + dot(lo, wide, 1, 0)) * scale

    for d in near:
        arrived(zA.at[0, NY * d], az_r.at[NY * d])
        for e in near:
            send_z(NY * d, NY * d + e)
    arrived(zB.at[2], bz_r.at[2])
    line_z(2, 3)
    line_z(2, 4)
    arrived(zB.at[6], bz_r.at[6])
    line_z(6, 5)
    for d in near:
        arrived(lrA.at[0, d], al_r.at[d])
        for e in near:
            send_l(d, NY * e + d)
    arrived(rlB.at[2], bl_r.at[2])
    line_l(2, 3)
    arrived(rlB.at[6], bl_r.at[6])
    line_l(6, 5)
    line_l(6, 4)

    columns = feat.shape[1] // 2
    ft[...] = dot(feat[:, pl.ds(pl.multiple_of(core * columns, columns), columns)], onehot, 0, 0).astype(BF16)
    acc[...] = jnp.zeros_like(acc)
    mass[...] = jnp.zeros_like(mass)
    norms_a(0, 0)
    norms_a(1, 0)
    for d in near:
        forward_z(NY * d).start()
        norms_a(0, NY * d)
    for j in (0, 2, 6, 1, 7, 3, 5, 4):
        if j in (1, 3, 4, 5, 7):
            arrived(zB.at[j], bz_r.at[j])
        norms_b(j)
    for j in (1, 7, 3, 5, 4):
        arrived(rlB.at[j], bl_r.at[j])

    def tile(h, n, count, j, blocks):
        rows = blocks * half
        zb = zB[pl.ds(j, blocks)].reshape(rows, embed)
        rl = rlB[pl.ds(j, blocks)].reshape(rows, embed)
        qb = qB[pl.ds(j, blocks)].reshape(rows, embed)
        za = zA[h, pl.ds(n, count)].reshape(count * half, embed)
        lr = lrA[h, pl.ds(n, count)].reshape(count * half, embed)
        qa = jnp.concatenate([qA[h, n + i, 0:1] for i in range(count)], axis=1)
        products = dot(zb, za, 1, 1)
        pairs = dot(rl, lr, 1, 1)
        weight = jnp.exp2(products * (2.0 * scale) - (jnp.concatenate([qb] * count, axis=1) + qa)) * pairs
        part = dot(weight.astype(BF16), za, 1, 0)
        acc[pl.ds(j, blocks)] += part.reshape(blocks, half, embed)
        row_mass = weight[:, :half]
        for i in range(1, count):
            row_mass = row_mass + weight[:, i * half:(i + 1) * half]
        mass[pl.ds(j, blocks)] += row_mass.reshape(blocks, half, embed)

    for d in (0, 1, 3, 2):
        for e in (0, 1, 3, 2):
            n = NY * d + e
            if e:
                arrived(zA.at[0, n], az_r.at[n])
                forward_z(n).start()
                norms_a(0, n)
            if n and not (d == 0):
                arrived(lrA.at[0, n], al_r.at[n])
            if n:
                forward_l(n).start()
        tile(0, NY * d, NY, 0, NZ)

    for n in range(1, PLANE):
        arrived(zA.at[1, n], fz_r.at[n])
        norms_a(1, n)
    for n in range(PLANE):
        arrived(lrA.at[1, n], fl_r.at[n])

    g_copies = [None] + [remote(gs.at[j], gr.at[j], g_s.at[j], g_r.at[j], at(0, 0, NZ - j, 0)) for j in range(1, NZ)]
    for j in (4, 2, 6, 0):
        tile(1, 0, PLANE, j, 2)
        for i in (j + 1, j):
            total = jnp.sum(mass[i], axis=1, keepdims=True)
            grad = (acc[i] - total * zB[i].astype(F32)) * (1.0 / embed)
            if i == 0:
                acc[0] = grad
            else:
                gs[i] = grad.astype(BF16)
                g_copies[i].start()

    for c in sends:
        c.wait_send()
    for n in range(PLANE):
        if n:
            forward_z(n).wait_send()
        forward_l(n).wait_send()

    grad = acc[0]
    for j in range(1, NZ):
        g_copies[j].wait_recv()
        grad = grad + gr[j].astype(F32)
    gfull[core] = grad
    gx = remote(gfull.at[core], gfull.at[core], gx_sem.at[0], gx_sem.at[1], sibling)
    gx.start()
    for j in range(1, NZ):
        g_copies[j].wait_send()
    gx.wait()

    both = gfull[...].reshape(2 * half, embed)
    embed_out[...] = both
    hi = both.astype(BF16)
    lo = (both - hi.astype(F32)).astype(BF16)
    wide = dot(ft[...], jnp.concatenate([hi, lo], axis=1), 1, 0)
    hp[...] = (wide[:, :embed] + wide[:, embed:]).astype(BF16).reshape(hp.shape)

    def slice_of(n):
        return ((x + n // NY) % NX) * NY + (y + n % NY) % NY

    hr_copies = [None] + [remote(hp.at[slice_of(n)], hr.at[n], hr_s.at[n], hr_r.at[n], plane_at(n)) for n in range(1, PLANE)]
    for n in range(1, PLANE):
        hr_copies[n].start()
    total = hp[me_plane].astype(F32)
    for n in range(1, PLANE):
        hr_copies[n].wait_recv()
        total = total + hr[n].astype(F32)
    hz[z] = (total * norm).astype(BF16)

    hz_copies = [None] + [remote(hz.at[z], hz.at[z], hz_s.at[j], hz_r.at[j], at(0, 0, j, 0)) for j in range(1, NZ)]
    for j in range(1, NZ):
        hz_copies[j].start()
    for n in range(1, PLANE):
        hr_copies[n].wait_send()
    for j in range(1, NZ):
        hz_copies[j].wait_recv()
    total = hz[0].astype(F32)
    for j in range(1, NZ):
        total = total + hz[j].astype(F32)
    hb[core, me_plane] = total.astype(BF16)

    ha_copies = [None] + [
        remote(hb.at[core, me_plane], hb.at[core, me_plane], ha_s.at[n], ha_r.at[n], plane_at(n)) for n in range(1, PLANE)]
    by_distance = sorted(range(PLANE), key=lambda n: min(n // NY, NX - n // NY) + min(n % NY, NY - n % NY))
    for n in by_distance[:0:-1]:
        ha_copies[n].start()
    hf_copies = []
    for n in by_distance:
        source = ((x + NX - n // NY) % NX) * NY + (y + NY - n % NY) % NY
        if n:
            ha_copies[n].wait_recv()
        c = remote(hb.at[core, source], hb.at[core, source], hf_s.at[n], hf_r.at[n], sibling)
        c.start()
        hf_copies.append(c)
    for j in range(1, NZ):
        hz_copies[j].wait_send()
    for n in range(1, PLANE):
        ha_copies[n].wait_send()
    for c in hf_copies:
        c.wait()
    head_out[...] = hb[...].reshape(head_out.shape)


def finish(head_in, embed_in, embed_out, head_out, head_v, head_f, embed_v, in_sem, out_sem):
    pieces = in_sem.shape[0] - 1
    rows = head_v.shape[0] // pieces
    cuts = [pl.ds(i * rows, rows) for i in range(pieces)]
    ins = [pltpu.make_async_copy(head_in.at[cut], head_v.at[cut], in_sem.at[i]) for i, cut in enumerate(cuts)]
    outs = [pltpu.make_async_copy(head_f.at[cut], head_out.at[cut], out_sem.at[i]) for i, cut in enumerate(cuts)]
    embed_load = pltpu.make_async_copy(embed_in, embed_v, in_sem.at[pieces])
    embed_store = pltpu.make_async_copy(embed_v, embed_out, out_sem.at[pieces])
    for c in ins:
        c.start()
    embed_load.start()
    for i, cut in enumerate(cuts):
        ins[i].wait()
        head_f[cut] = head_v[cut].astype(F32)
        outs[i].start()
    embed_load.wait()
    embed_store.start()
    for c in outs:
        c.wait()
    embed_store.wait()


def local(batch_index, chip_features, head_weight, probe_left, probe_right):
    points = batch_index.shape[0]
    half = points // 2
    chips, width = chip_features.shape
    probes = probe_left.shape[1]
    embed = head_weight.shape[1]
    rows = width // 2 // PLANE
    norm = 1.0 / math.sqrt(points * PLANE * NZ)
    block = (half, embed)
    vmem, dma = pltpu.VMEM, pltpu.SemaphoreType.DMA
    head, grad = pl.pallas_call(
        functools.partial(fused, norm),
        out_shape=(jax.ShapeDtypeStruct((width, embed), BF16), jax.ShapeDtypeStruct((points, embed), F32)),
        in_specs=[pl.BlockSpec(memory_space=pl.ANY)] * 5,
        out_specs=[pl.BlockSpec(memory_space=pltpu.VMEM)] * 2,
        scratch_shapes=[
            vmem((points,), jnp.int32), vmem((probes, points), BF16), vmem((probes, points), BF16),
            vmem((chips, width), BF16), vmem((width, embed), BF16), vmem((chips, embed), BF16),
            vmem((width // 2, points), BF16), vmem((2, 2) + block, BF16), vmem((2,) + block, BF16),
            vmem((2,) + block, BF16), vmem((2, PLANE) + block, BF16), vmem((2, PLANE) + block, BF16),
            vmem((2, PLANE, 8, half), F32), vmem((NZ,) + block, BF16), vmem((NZ,) + block, BF16),
            vmem((NZ,) + block, F32), vmem((NZ,) + block, F32), vmem((NZ,) + block, F32),
            vmem((NZ,) + block, BF16), vmem((NZ,) + block, BF16), vmem((2,) + block, F32),
            vmem((PLANE, rows, embed), BF16), vmem((PLANE, rows, embed), BF16),
            vmem((NZ, rows, embed), BF16), vmem((2, PLANE, rows, embed), BF16),
            dma((4,)), dma((4,)), dma((2,)),
            dma((PLANE,)), dma((PLANE,)), dma((PLANE,)), dma((PLANE,)),
            dma((PLANE,)), dma((PLANE,)), dma((PLANE,)), dma((PLANE,)),
            dma((NZ,)), dma((NZ,)), dma((NZ,)), dma((NZ,)), dma((NZ,)), dma((NZ,)), dma((2,)),
            dma((PLANE,)), dma((PLANE,)), dma((NZ,)), dma((NZ,)),
            dma((PLANE,)), dma((PLANE,)), dma((PLANE,)), dma((PLANE,)),
        ],
        compiler_params=pltpu.CompilerParams(
            collective_id=0, has_side_effects=True, vmem_limit_bytes=60 * 2**20),
    )(batch_index, chip_features, head_weight, probe_left.T, probe_right.T)
    return pl.pallas_call(
        finish,
        out_shape=(jax.ShapeDtypeStruct((points, embed), F32), jax.ShapeDtypeStruct((width, embed), F32)),
        in_specs=[pl.BlockSpec(memory_space=pl.ANY)] * 2,
        out_specs=[pl.BlockSpec(memory_space=pl.ANY)] * 2,
        scratch_shapes=[
            vmem((width, embed), BF16), vmem((width, embed), F32), vmem((points, embed), F32), dma((5,)), dma((5,))],
    )(head, grad)


def solution(mesh):
    return jax.shard_map(
        local,
        mesh=mesh,
        in_specs=(P(("row", "col")), P(("row", "col"), None), P(), P(("row", "col"), "cores"), P(("row", "col"), "cores")),
        out_specs=(P(("row", "col"), None), P()),
        check_vma=False,
    )
```

```python
import functools
import math

import jax
import jax.numpy as jnp
from jax import lax
from jax.experimental import pallas as pl
from jax.experimental.pallas import tpu as pltpu
from jax.sharding import PartitionSpec as P

MESH = pl.DeviceIdType.MESH
F32, BF16 = jnp.float32, jnp.bfloat16
NX, NY, NZ = 4, 4, 8
PLANE = NX * NY


def dot(a, b, ca, cb):
    return lax.dot_general(a, b, (((ca,), (cb,)), ((), ())), preferred_element_type=F32)


def squares(z):
    zf = z.astype(F32)
    sq = zf * zf
    hi = sq.astype(BF16)
    return hi, (sq - hi.astype(F32)).astype(BF16)


def fused(norm, idx_hbm, feat_hbm, w_hbm, left_hbm, right_hbm, head_out, embed_out,
          idx_ref, left_ref, right_ref, feat, w, e_all, ft, u_buf, u_in, z_own, zA, lrA, qA, zB, rlB, qB, acc, mass,
          gs, gr, gfull, hp, hr, hz, hb,
          feat_sem, in_sem, u_sem, az_s, az_r, al_s, al_r, fz_s, fz_r, fl_s, fl_r,
          bz_s, bz_r, bl_s, bl_r, g_s, g_r, gx_sem, hr_s, hr_r, hz_s, hz_r, ha_s, ha_r, hf_s, hf_r):
    row, col, core = lax.axis_index("row"), lax.axis_index("col"), lax.axis_index("cores")
    x, y, z = (row // NZ) * 2 + col // NY, col % NY, row % NZ
    half = z_own.shape[1]
    embed = z_own.shape[2]
    scale = 0.5 / embed * math.log2(math.e)

    def at(dx, dy, dz, dc):
        nx, ny, nz = (x + dx) % NX, (y + dy) % NY, (z + dz) % NZ
        return ((nx // 2) * NZ + nz, (nx % 2) * NY + ny, (core + dc) % 2)

    def plane_at(n):
        return at(n // NY, n % NY, 0, 0)

    def remote(src, dst, ssem, rsem, device):
        return pltpu.make_async_remote_copy(
            src_ref=src, dst_ref=dst, send_sem=ssem, recv_sem=rsem, device_id=device, device_id_type=MESH)

    sibling = at(0, 0, 0, 1)
    me_plane = x * NY + y
    other = 1 - core

    near = (1, 3, 2)
    axes = [0] + [NY * d for d in near] + list(near)
    diagonal = [NY * d + e for d in near for e in near]
    order = axes + [PLANE + n for n in axes] + diagonal + [PLANE + n for n in diagonal]
    own = [order.index(n) for n in range(PLANE)]
    passed = [order.index(PLANE + n) for n in range(PLANE)]
    line = [(j + NZ // 2) % NZ for j in range(NZ)]
    early = 2 * len(axes)

    chunk = feat.shape[0] // 4
    small_copies = [
        pltpu.make_async_copy(src, dst, in_sem.at[i])
        for i, (src, dst) in enumerate(((left_hbm, left_ref), (right_hbm, right_ref), (idx_hbm, idx_ref), (w_hbm, w)))]
    for c in small_copies:
        c.start()
    feat_copies = [
        pltpu.make_async_copy(feat_hbm.at[pl.ds(i * chunk, chunk)], feat.at[pl.ds(i * chunk, chunk)], feat_sem.at[i])
        for i in range(4)]
    for c in feat_copies:
        c.start()

    barrier = pltpu.get_barrier_semaphore()
    for n in range(1, PLANE):
        pl.semaphore_signal(barrier, inc=1, device_id=plane_at(n), device_id_type=MESH)
    for j in range(1, NZ):
        pl.semaphore_signal(barrier, inc=1, device_id=at(0, 0, j, 0), device_id_type=MESH)
    pl.semaphore_signal(barrier, inc=1, device_id=sibling, device_id_type=MESH)

    probes = left_ref.shape[0]
    lane = lax.broadcasted_iota(jnp.int32, (probes, embed), 1)
    sub = lax.broadcasted_iota(jnp.int32, (probes, embed), 0)
    first = (lane == sub + 2 * probes * core).astype(F32).astype(BF16)
    second = (lane == sub + 2 * probes * core + probes).astype(F32).astype(BF16)
    small_copies[0].wait()
    small_copies[1].wait()
    lv, rv = left_ref[...], right_ref[...]
    u = (dot(lv, first, 0, 0) + dot(rv, second, 0, 0)).astype(BF16)
    v = (dot(lv, second, 0, 0) + dot(rv, first, 0, 0)).astype(BF16)
    for h in range(2):
        u_buf[h, 0] = u[h * half:(h + 1) * half]
        u_buf[h, 1] = v[h * half:(h + 1) * half]

    small_copies[3].wait()
    for i, c in enumerate(feat_copies):
        c.wait()
        e_all[pl.ds(i * chunk, chunk)] = dot(feat[pl.ds(i * chunk, chunk)], w[...], 1, 0).astype(BF16)

    pl.semaphore_wait(barrier, PLANE - 1 + NZ - 1 + 1)

    sends = []

    def send(src, dst, ssem, rsem, device):
        c = remote(src, dst, ssem, rsem, device)
        c.start()
        sends.append(c)
        return c

    u_copy = send(u_buf.at[other], u_in, u_sem.at[0], u_sem.at[1], sibling)

    small_copies[2].wait()
    index = idx_ref[...].reshape(1, 2 * half)
    onehot = (lax.broadcasted_iota(jnp.int32, (feat.shape[0], 2 * half), 0) == index).astype(F32).astype(BF16)
    z_all = dot(onehot, e_all[...], 0, 0).astype(BF16)
    z_own[0] = z_all[:half]
    z_own[1] = z_all[half:]
    mine = z_own[core]
    zA[own[0]] = mine
    zA[passed[0]] = z_own[other]
    zB[line[0]] = mine

    def send_z(n, m):
        return send(zA.at[own[n]], zA.at[own[m]], az_s.at[m], az_r.at[m], plane_at(m - n))

    def send_l(n, m):
        return send(lrA.at[own[n]], lrA.at[own[m]], al_s.at[m], al_r.at[m], plane_at(m - n))

    def line_z(i, j):
        return send(zB.at[line[i]], zB.at[line[j]], bz_s.at[j], bz_r.at[j], at(0, 0, (j - i) % NZ, 0))

    def line_l(i, j):
        return send(rlB.at[line[i]], rlB.at[line[j]], bl_s.at[j], bl_r.at[j], at(0, 0, (j - i) % NZ, 0))

    def arrived(buf, sem):
        remote(buf, buf, sem, sem, sibling).wait_recv()

    for d in near:
        send_z(0, NY * d)
    line_z(0, 2)
    line_z(0, 6)
    for d in near:
        send_z(0, d)
    line_z(0, 1)
    line_z(0, 7)
    u_copy.wait_recv()
    lrA[own[0]] = u_buf[core, 0] + u_in[0]
    rlB[line[0]] = u_buf[core, 1] + u_in[1]
    for d in near:
        send_l(0, d)
    line_l(0, 2)
    line_l(0, 6)
    for d in near:
        send_l(0, NY * d)
    line_l(0, 1)
    line_l(0, 7)

    def forward_z(n):
        return remote(zA.at[own[n]], zA.at[passed[n]], fz_s.at[n], fz_r.at[n], sibling)

    def forward_l(n):
        return remote(lrA.at[own[n]], lrA.at[passed[n]], fl_s.at[n], fl_r.at[n], sibling)

    forward_l(0).start()
    ones = jnp.ones((8, embed), BF16)
    wide = jnp.ones((embed, embed), BF16)

    def norms_a(p, count):
        hi, lo = squares(zA[p:p + count].reshape(count * half, embed))
        q = (dot(ones, hi, 1, 1) + dot(ones, lo, 1, 1)) * scale
        for i in range(count):
            qA[p + i] = q[:, i * half:(i + 1) * half]

    def norms_b(p, count):
        hi, lo = squares(zB[p:p + count].reshape(count * half, embed))
        qB[p:p + count] = ((dot(hi, wide, 1, 0) + dot(lo, wide, 1, 0)) * scale).reshape(count, half, embed)

    for d in near:
        arrived(zA.at[own[NY * d]], az_r.at[NY * d])
        for e in near:
            send_z(NY * d, NY * d + e)
        forward_z(NY * d).start()
    arrived(zB.at[line[2]], bz_r.at[2])
    line_z(2, 3)
    line_z(2, 4)
    arrived(zB.at[line[6]], bz_r.at[6])
    line_z(6, 5)
    for d in near:
        arrived(lrA.at[own[d]], al_r.at[d])
        for e in near:
            send_l(d, NY * e + d)
        forward_l(d).start()
    arrived(rlB.at[line[2]], bl_r.at[2])
    line_l(2, 3)
    arrived(rlB.at[line[6]], bl_r.at[6])
    line_l(6, 5)
    line_l(6, 4)
    for d in near:
        arrived(zA.at[own[d]], az_r.at[d])
        forward_z(d).start()
        arrived(lrA.at[own[NY * d]], al_r.at[NY * d])
        forward_l(NY * d).start()
    for j in (1, 7):
        arrived(zB.at[line[j]], bz_r.at[j])
        arrived(rlB.at[line[j]], bl_r.at[j])

    def tile(p, count, s, blocks, first):
        rows = blocks * half
        zb = zB[s:s + blocks].reshape(rows, embed)
        rl = rlB[s:s + blocks].reshape(rows, embed)
        qb = qB[s:s + blocks].reshape(rows, embed)
        za = zA[p:p + count].reshape(count * half, embed)
        lr = lrA[p:p + count].reshape(count * half, embed)
        qa = jnp.concatenate([qA[p + i, 0:1] for i in range(count)], axis=1)
        products = dot(zb, za, 1, 1)
        pairs = dot(rl, lr, 1, 1)
        weight = jnp.exp2(products * (2.0 * scale) - (jnp.concatenate([qb] * count, axis=1) + qa)) * pairs
        part = dot(weight.astype(BF16), za, 1, 0).reshape(blocks, half, embed)
        row_mass = weight[:, :half]
        for i in range(1, count):
            row_mass = row_mass + weight[:, i * half:(i + 1) * half]
        row_mass = row_mass.reshape(blocks, half, embed)
        if first:
            acc[s:s + blocks] = part
            mass[s:s + blocks] = row_mass
        else:
            acc[s:s + blocks] += part
            mass[s:s + blocks] += row_mass

    norms_b(line[6], 4)
    norms_a(0, len(axes))
    for n in axes:
        if n:
            arrived(zA.at[passed[n]], fz_r.at[n])
        arrived(lrA.at[passed[n]], fl_r.at[n])
    norms_a(len(axes), len(axes))
    tile(0, early, line[6], 4, True)

    for n in diagonal:
        arrived(zA.at[own[n]], az_r.at[n])
        forward_z(n).start()
        arrived(lrA.at[own[n]], al_r.at[n])
        forward_l(n).start()
    norms_a(early, len(diagonal))
    for j in (3, 5, 4):
        arrived(zB.at[line[j]], bz_r.at[j])
        arrived(rlB.at[line[j]], bl_r.at[j])
    norms_b(line[4], 2)
    norms_b(line[2], 2)
    tile(0, early, line[4], 2, True)
    for n in diagonal:
        arrived(zA.at[passed[n]], fz_r.at[n])
        arrived(lrA.at[passed[n]], fl_r.at[n])
    norms_a(early + len(diagonal), len(diagonal))

    g_copies = [None] + [remote(gs.at[j], gr.at[j], g_s.at[j], g_r.at[j], at(0, 0, NZ - j, 0)) for j in range(1, NZ)]
    for j in (4, 2, 6, 0):
        s = line[j]
        if j == 2:
            tile(0, early, s, 2, True)
        tile(early, 2 * len(diagonal), s, 2, False)
        for i in (1, 0):
            total = jnp.sum(mass[s + i], axis=1, keepdims=True)
            grad = (acc[s + i] - total * zB[s + i].astype(F32)) * (1.0 / embed)
            if j + i == 0:
                acc[s] = grad
            else:
                gs[j + i] = grad.astype(BF16)
                g_copies[j + i].start()

    columns = feat.shape[1] // 2
    mine_t = feat[:, pl.ds(pl.multiple_of(core * columns, columns), columns)]
    ft[...] = dot(mine_t, onehot, 0, 0).astype(BF16)

    for c in sends:
        c.wait_send()
    for n in range(PLANE):
        if n:
            forward_z(n).wait_send()
        forward_l(n).wait_send()

    grad = acc[line[0]]
    for j in range(1, NZ):
        g_copies[j].wait_recv()
        grad = grad + gr[j].astype(F32)
    gfull[core] = grad
    gx = remote(gfull.at[core], gfull.at[core], gx_sem.at[0], gx_sem.at[1], sibling)
    gx.start()

    def head_product(which, value):
        hi = value.astype(BF16)
        lo = (value - hi.astype(F32)).astype(BF16)
        lanes = pl.ds(pl.multiple_of(which * half, half), half)
        return dot(ft[:, lanes], jnp.concatenate([hi, lo], axis=1), 1, 0)

    mine = head_product(core, grad)
    for j in range(1, NZ):
        g_copies[j].wait_send()
    gx.wait()
    product = mine + head_product(other, gfull[other])
    hp[...] = (product[:, :embed] + product[:, embed:]).astype(BF16).reshape(hp.shape)

    def slice_of(n):
        return ((x + n // NY) % NX) * NY + (y + n % NY) % NY

    hr_copies = [None] + [remote(hp.at[slice_of(n)], hr.at[n], hr_s.at[n], hr_r.at[n], plane_at(n)) for n in range(1, PLANE)]
    by_distance = sorted(range(PLANE), key=lambda n: min(n // NY, NX - n // NY) + min(n % NY, NY - n % NY))
    for n in by_distance[:0:-1]:
        hr_copies[n].start()
    embed_out[...] = gfull[...].reshape(2 * half, embed)
    total = hp[me_plane].astype(F32)
    for n in by_distance[1:]:
        hr_copies[n].wait_recv()
        total = total + hr[n].astype(F32)
    hz[z] = (total * norm).astype(BF16)

    hz_copies = [None] + [remote(hz.at[z], hz.at[z], hz_s.at[j], hz_r.at[j], at(0, 0, j, 0)) for j in range(1, NZ)]
    for j in range(1, NZ):
        hz_copies[j].start()
    for n in range(1, PLANE):
        hr_copies[n].wait_send()
    for j in range(1, NZ):
        hz_copies[j].wait_recv()
    total = hz[0].astype(F32)
    for j in range(1, NZ):
        total = total + hz[j].astype(F32)
    hb[core, me_plane] = total.astype(BF16)

    ha_copies = [None] + [
        remote(hb.at[core, me_plane], hb.at[core, me_plane], ha_s.at[n], ha_r.at[n], plane_at(n)) for n in range(1, PLANE)]
    for n in by_distance[:0:-1]:
        ha_copies[n].start()
    hf_copies = []
    for n in by_distance:
        source = ((x + NX - n // NY) % NX) * NY + (y + NY - n % NY) % NY
        if n:
            ha_copies[n].wait_recv()
        c = remote(hb.at[core, source], hb.at[core, source], hf_s.at[n], hf_r.at[n], sibling)
        c.start()
        hf_copies.append(c)
    for j in range(1, NZ):
        hz_copies[j].wait_send()
    for n in range(1, PLANE):
        ha_copies[n].wait_send()
    for c in hf_copies:
        c.wait()
    head_out[...] = hb[...].reshape(head_out.shape)


def finish(head_in, embed_in, embed_out, head_out, head_f, out_sem):
    pieces = out_sem.shape[0] - 1
    rows = head_f.shape[0] // pieces
    embed_store = pltpu.make_async_copy(embed_in, embed_out, out_sem.at[pieces])
    embed_store.start()
    stores = []
    for i in range(pieces):
        cut = pl.ds(i * rows, rows)
        head_f[cut] = head_in[cut].astype(F32)
        stores.append(pltpu.make_async_copy(head_f.at[cut], head_out.at[cut], out_sem.at[i]))
        stores[i].start()
    for c in stores:
        c.wait()
    embed_store.wait()


def local(batch_index, chip_features, head_weight, probe_left, probe_right):
    points = batch_index.shape[0]
    half = points // 2
    chips, width = chip_features.shape
    probes = probe_left.shape[1]
    embed = head_weight.shape[1]
    rows = width // 2 // PLANE
    norm = 1.0 / math.sqrt(points * PLANE * NZ)
    block = (half, embed)
    vmem, dma = pltpu.VMEM, pltpu.SemaphoreType.DMA
    head, grad = pl.pallas_call(
        functools.partial(fused, norm),
        out_shape=(jax.ShapeDtypeStruct((width, embed), BF16), jax.ShapeDtypeStruct((points, embed), F32)),
        in_specs=[pl.BlockSpec(memory_space=pl.ANY)] * 5,
        out_specs=[pl.BlockSpec(memory_space=pltpu.VMEM)] * 2,
        scratch_shapes=[
            vmem((points,), jnp.int32), vmem((probes, points), BF16), vmem((probes, points), BF16),
            vmem((chips, width), BF16), vmem((width, embed), BF16), vmem((chips, embed), BF16),
            vmem((width // 2, points), BF16), vmem((2, 2) + block, BF16), vmem((2,) + block, BF16),
            vmem((2,) + block, BF16), vmem((2 * PLANE,) + block, BF16), vmem((2 * PLANE,) + block, BF16),
            vmem((2 * PLANE, 8, half), F32), vmem((NZ,) + block, BF16), vmem((NZ,) + block, BF16),
            vmem((NZ,) + block, F32), vmem((NZ,) + block, F32), vmem((NZ,) + block, F32),
            vmem((NZ,) + block, BF16), vmem((NZ,) + block, BF16), vmem((2,) + block, F32),
            vmem((PLANE, rows, embed), BF16), vmem((PLANE, rows, embed), BF16),
            vmem((NZ, rows, embed), BF16), vmem((2, PLANE, rows, embed), BF16),
            dma((4,)), dma((4,)), dma((2,)),
            dma((PLANE,)), dma((PLANE,)), dma((PLANE,)), dma((PLANE,)),
            dma((PLANE,)), dma((PLANE,)), dma((PLANE,)), dma((PLANE,)),
            dma((NZ,)), dma((NZ,)), dma((NZ,)), dma((NZ,)), dma((NZ,)), dma((NZ,)), dma((2,)),
            dma((PLANE,)), dma((PLANE,)), dma((NZ,)), dma((NZ,)),
            dma((PLANE,)), dma((PLANE,)), dma((PLANE,)), dma((PLANE,)),
        ],
        compiler_params=pltpu.CompilerParams(
            collective_id=0, has_side_effects=True, vmem_limit_bytes=48 * 2**20),
    )(*(pltpu.with_memory_space_constraint(a, pltpu.HBM)
        for a in (batch_index, chip_features, head_weight, probe_left.T, probe_right.T)))
    return pl.pallas_call(
        finish,
        out_shape=(jax.ShapeDtypeStruct((points, embed), F32), jax.ShapeDtypeStruct((width, embed), F32)),
        in_specs=[pl.BlockSpec(memory_space=pltpu.VMEM)] * 2,
        out_specs=[pl.BlockSpec(memory_space=pl.ANY)] * 2,
        scratch_shapes=[vmem((width, embed), F32), dma((5,))],
        compiler_params=pltpu.CompilerParams(vmem_limit_bytes=4 * 2**20),
    )(head, grad)


def solution(mesh):
    return jax.shard_map(
        local,
        mesh=mesh,
        in_specs=(P(("row", "col")), P(("row", "col"), None), P(), P(("row", "col"), "cores"), P(("row", "col"), "cores")),
        out_specs=(P(("row", "col"), None), P()),
        check_vma=False,
    )
```

```python
import functools
import math

import jax
import jax.numpy as jnp
from jax import lax
from jax.experimental import pallas as pl
from jax.experimental.pallas import tpu as pltpu
from jax.sharding import PartitionSpec as P

MESH = pl.DeviceIdType.MESH
F32, BF16 = jnp.float32, jnp.bfloat16
NX, NY, NZ = 4, 4, 8
PLANE = NX * NY


def dot(a, b, ca, cb):
    return lax.dot_general(a, b, (((ca,), (cb,)), ((), ())), preferred_element_type=F32)


def squares(z):
    zf = z.astype(F32)
    sq = zf * zf
    hi = sq.astype(BF16)
    return hi, (sq - hi.astype(F32)).astype(BF16)


def fused(norm, idx_hbm, feat_hbm, w_hbm, left_hbm, right_hbm, head_out, embed_out,
          idx_ref, left_ref, right_ref, feat, w, e_all, ft, u_buf, u_in, z_own, zA, lrA, qA, zB, rlB, qB, acc, mass,
          gs, gr, gfull, hp, hr, hz, hb,
          feat_sem, in_sem, u_sem, az_s, az_r, al_s, al_r, fz_s, fz_r, fl_s, fl_r,
          bz_s, bz_r, bl_s, bl_r, g_s, g_r, gx_sem, hr_s, hr_r, hz_s, hz_r, ha_s, ha_r, hf_s, hf_r):
    row, col, core = lax.axis_index("row"), lax.axis_index("col"), lax.axis_index("cores")
    x, y, z = (row // NZ) * 2 + col // NY, col % NY, row % NZ
    half = z_own.shape[1]
    embed = z_own.shape[2]
    scale = 0.5 / embed * math.log2(math.e)

    def at(dx, dy, dz, dc):
        nx, ny, nz = (x + dx) % NX, (y + dy) % NY, (z + dz) % NZ
        return ((nx // 2) * NZ + nz, (nx % 2) * NY + ny, (core + dc) % 2)

    def plane_at(n):
        return at(n // NY, n % NY, 0, 0)

    def remote(src, dst, ssem, rsem, device):
        return pltpu.make_async_remote_copy(
            src_ref=src, dst_ref=dst, send_sem=ssem, recv_sem=rsem, device_id=device, device_id_type=MESH)

    sibling = at(0, 0, 0, 1)
    me_plane = x * NY + y
    other = 1 - core

    near = (1, 3, 2)
    axes = [0] + [NY * d for d in near] + list(near)
    diagonal = [NY * d + e for d in near for e in near]
    order = axes + [PLANE + n for n in axes] + diagonal + [PLANE + n for n in diagonal]
    own = [order.index(n) for n in range(PLANE)]
    passed = [order.index(PLANE + n) for n in range(PLANE)]
    line = [(j + NZ // 2) % NZ for j in range(NZ)]
    early = 2 * len(axes)

    chunk = feat.shape[0] // 4
    small_copies = [
        pltpu.make_async_copy(src, dst, in_sem.at[i])
        for i, (src, dst) in enumerate(((left_hbm, left_ref), (right_hbm, right_ref), (idx_hbm, idx_ref), (w_hbm, w)))]
    for c in small_copies:
        c.start()
    feat_copies = [
        pltpu.make_async_copy(feat_hbm.at[pl.ds(i * chunk, chunk)], feat.at[pl.ds(i * chunk, chunk)], feat_sem.at[i])
        for i in range(4)]
    for c in feat_copies:
        c.start()

    barrier = pltpu.get_barrier_semaphore()
    for n in range(1, PLANE):
        pl.semaphore_signal(barrier, inc=1, device_id=plane_at(n), device_id_type=MESH)
    for j in range(1, NZ):
        pl.semaphore_signal(barrier, inc=1, device_id=at(0, 0, j, 0), device_id_type=MESH)
    pl.semaphore_signal(barrier, inc=1, device_id=sibling, device_id_type=MESH)

    probes = left_ref.shape[0]
    lane = lax.broadcasted_iota(jnp.int32, (probes, embed), 1)
    sub = lax.broadcasted_iota(jnp.int32, (probes, embed), 0)
    first = (lane == sub + 2 * probes * core).astype(F32).astype(BF16)
    second = (lane == sub + 2 * probes * core + probes).astype(F32).astype(BF16)
    small_copies[0].wait()
    small_copies[1].wait()
    lv, rv = left_ref[...], right_ref[...]
    u = (dot(lv, first, 0, 0) + dot(rv, second, 0, 0)).astype(BF16)
    v = (dot(lv, second, 0, 0) + dot(rv, first, 0, 0)).astype(BF16)
    for h in range(2):
        u_buf[h, 0] = u[h * half:(h + 1) * half]
        u_buf[h, 1] = v[h * half:(h + 1) * half]

    small_copies[3].wait()
    for i, c in enumerate(feat_copies):
        c.wait()
        e_all[pl.ds(i * chunk, chunk)] = dot(feat[pl.ds(i * chunk, chunk)], w[...], 1, 0).astype(BF16)

    pl.semaphore_wait(barrier, PLANE - 1 + NZ - 1 + 1)

    sends = []

    def send(src, dst, ssem, rsem, device):
        c = remote(src, dst, ssem, rsem, device)
        c.start()
        sends.append(c)
        return c

    u_copy = send(u_buf.at[other], u_in, u_sem.at[0], u_sem.at[1], sibling)

    small_copies[2].wait()
    index = idx_ref[...].reshape(1, 2 * half)
    onehot = (lax.broadcasted_iota(jnp.int32, (feat.shape[0], 2 * half), 0) == index).astype(F32).astype(BF16)
    z_all = dot(onehot, e_all[...], 0, 0).astype(BF16)
    z_own[0] = z_all[:half]
    z_own[1] = z_all[half:]
    mine = z_own[core]
    zA[own[0]] = mine
    zA[passed[0]] = z_own[other]
    zB[line[0]] = mine

    def send_z(n, m):
        return send(zA.at[own[n]], zA.at[own[m]], az_s.at[m], az_r.at[m], plane_at(m - n))

    def send_l(n, m):
        return send(lrA.at[own[n]], lrA.at[own[m]], al_s.at[m], al_r.at[m], plane_at(m - n))

    def line_z(i, j):
        return send(zB.at[line[i]], zB.at[line[j]], bz_s.at[j], bz_r.at[j], at(0, 0, (j - i) % NZ, 0))

    def line_l(i, j):
        return send(rlB.at[line[i]], rlB.at[line[j]], bl_s.at[j], bl_r.at[j], at(0, 0, (j - i) % NZ, 0))

    def arrived(buf, sem):
        remote(buf, buf, sem, sem, sibling).wait_recv()

    for d in near:
        send_z(0, NY * d)
    line_z(0, 2)
    line_z(0, 6)
    for d in near:
        send_z(0, d)
    line_z(0, 1)
    line_z(0, 7)
    u_copy.wait_recv()
    lrA[own[0]] = u_buf[core, 0] + u_in[0]
    rlB[line[0]] = u_buf[core, 1] + u_in[1]
    for d in near:
        send_l(0, d)
    line_l(0, 2)
    line_l(0, 6)
    for d in near:
        send_l(0, NY * d)
    line_l(0, 1)
    line_l(0, 7)

    def forward_z(n):
        return remote(zA.at[own[n]], zA.at[passed[n]], fz_s.at[n], fz_r.at[n], sibling)

    def forward_l(n):
        return remote(lrA.at[own[n]], lrA.at[passed[n]], fl_s.at[n], fl_r.at[n], sibling)

    forward_l(0).start()
    ones = jnp.ones((8, embed), BF16)
    wide = jnp.ones((embed, embed), BF16)

    def norms_a(p, count):
        hi, lo = squares(zA[p:p + count].reshape(count * half, embed))
        q = (dot(ones, hi, 1, 1) + dot(ones, lo, 1, 1)) * scale
        for i in range(count):
            qA[p + i] = q[:, i * half:(i + 1) * half]

    def norms_b(p, count):
        hi, lo = squares(zB[p:p + count].reshape(count * half, embed))
        qB[p:p + count] = ((dot(hi, wide, 1, 0) + dot(lo, wide, 1, 0)) * scale).reshape(count, half, embed)

    for d in near:
        arrived(zA.at[own[NY * d]], az_r.at[NY * d])
        for e in near:
            send_z(NY * d, NY * d + e)
        forward_z(NY * d).start()
    arrived(zB.at[line[2]], bz_r.at[2])
    line_z(2, 3)
    line_z(2, 4)
    arrived(zB.at[line[6]], bz_r.at[6])
    line_z(6, 5)
    for d in near:
        arrived(lrA.at[own[d]], al_r.at[d])
        for e in near:
            send_l(d, NY * e + d)
        forward_l(d).start()
    arrived(rlB.at[line[2]], bl_r.at[2])
    line_l(2, 3)
    arrived(rlB.at[line[6]], bl_r.at[6])
    line_l(6, 5)
    line_l(6, 4)
    for d in near:
        arrived(zA.at[own[d]], az_r.at[d])
        forward_z(d).start()
        arrived(lrA.at[own[NY * d]], al_r.at[NY * d])
        forward_l(NY * d).start()
    for j in (1, 7):
        arrived(zB.at[line[j]], bz_r.at[j])
        arrived(rlB.at[line[j]], bl_r.at[j])

    def tile(p, count, s, blocks, first):
        rows = blocks * half
        zb = zB[s:s + blocks].reshape(rows, embed)
        rl = rlB[s:s + blocks].reshape(rows, embed)
        qb = qB[s:s + blocks].reshape(rows, embed)
        za = zA[p:p + count].reshape(count * half, embed)
        lr = lrA[p:p + count].reshape(count * half, embed)
        qa = jnp.concatenate([qA[p + i, 0:1] for i in range(count)], axis=1)
        products = dot(zb, za, 1, 1)
        pairs = dot(rl, lr, 1, 1)
        weight = jnp.exp2(products * (2.0 * scale) - (jnp.concatenate([qb] * count, axis=1) + qa)) * pairs
        part = dot(weight.astype(BF16), za, 1, 0).reshape(blocks, half, embed)
        row_mass = weight[:, :half]
        for i in range(1, count):
            row_mass = row_mass + weight[:, i * half:(i + 1) * half]
        row_mass = row_mass.reshape(blocks, half, embed)
        if first:
            acc[s:s + blocks] = part
            mass[s:s + blocks] = row_mass
        else:
            acc[s:s + blocks] += part
            mass[s:s + blocks] += row_mass

    norms_b(line[6], 4)
    norms_a(0, len(axes))
    for n in axes:
        if n:
            arrived(zA.at[passed[n]], fz_r.at[n])
        arrived(lrA.at[passed[n]], fl_r.at[n])
    norms_a(len(axes), len(axes))
    tile(0, early, line[6], 4, True)

    columns = feat.shape[1] // 2
    mine_t = feat[:, pl.ds(pl.multiple_of(core * columns, columns), columns)]
    ft[...] = dot(mine_t, onehot, 0, 0).astype(BF16)


    for n in diagonal:
        arrived(zA.at[own[n]], az_r.at[n])
        forward_z(n).start()
        arrived(lrA.at[own[n]], al_r.at[n])
        forward_l(n).start()
    norms_a(early, len(diagonal))
    for j in (3, 5, 4):
        arrived(zB.at[line[j]], bz_r.at[j])
        arrived(rlB.at[line[j]], bl_r.at[j])
    norms_b(line[4], 2)
    norms_b(line[2], 2)
    tile(0, early, line[4], 2, True)
    for n in diagonal:
        arrived(zA.at[passed[n]], fz_r.at[n])
        arrived(lrA.at[passed[n]], fl_r.at[n])
    norms_a(early + len(diagonal), len(diagonal))

    g_copies = [None] + [remote(gs.at[j], gr.at[j], g_s.at[j], g_r.at[j], at(0, 0, NZ - j, 0)) for j in range(1, NZ)]
    for j in (4, 2, 6, 0):
        s = line[j]
        if j == 2:
            tile(0, early, s, 2, True)
        tile(early, 2 * len(diagonal), s, 2, False)
        for i in (1, 0):
            total = jnp.sum(mass[s + i], axis=1, keepdims=True)
            grad = (acc[s + i] - total * zB[s + i].astype(F32)) * (1.0 / embed)
            if j + i == 0:
                acc[s] = grad
            else:
                gs[j + i] = grad.astype(BF16)
                g_copies[j + i].start()

    grad = acc[line[0]]
    for j in range(1, NZ):
        g_copies[j].wait_recv()
        grad = grad + gr[j].astype(F32)
    gfull[core] = grad
    gx = remote(gfull.at[core], gfull.at[core], gx_sem.at[0], gx_sem.at[1], sibling)
    gx.start()

    def head_product(which, value):
        hi = value.astype(BF16)
        lo = (value - hi.astype(F32)).astype(BF16)
        lanes = pl.ds(pl.multiple_of(which * half, half), half)
        return dot(ft[:, lanes], jnp.concatenate([hi, lo], axis=1), 1, 0)

    mine = head_product(core, grad)
    for j in range(1, NZ):
        g_copies[j].wait_send()
    gx.wait()
    product = mine + head_product(other, gfull[other])
    hp[...] = (product[:, :embed] + product[:, embed:]).astype(BF16).reshape(hp.shape)

    def slice_of(n):
        return ((x + n // NY) % NX) * NY + (y + n % NY) % NY

    hr_copies = [None] + [remote(hp.at[slice_of(n)], hr.at[n], hr_s.at[n], hr_r.at[n], plane_at(n)) for n in range(1, PLANE)]
    by_distance = sorted(range(PLANE), key=lambda n: min(n // NY, NX - n // NY) + min(n % NY, NY - n % NY))
    for n in by_distance[:0:-1]:
        hr_copies[n].start()
    embed_out[...] = gfull[...].reshape(2 * half, embed)

    for c in sends:
        c.wait_send()
    for n in range(PLANE):
        if n:
            forward_z(n).wait_send()
        forward_l(n).wait_send()

    total = hp[me_plane].astype(F32)
    for n in by_distance[1:]:
        hr_copies[n].wait_recv()
        total = total + hr[n].astype(F32)
    hz[z] = (total * norm).astype(BF16)

    hz_copies = [None] + [remote(hz.at[z], hz.at[z], hz_s.at[j], hz_r.at[j], at(0, 0, j, 0)) for j in range(1, NZ)]
    for j in (4, 3, 5, 2, 6, 1, 7):
        hz_copies[j].start()
    for n in range(1, PLANE):
        hr_copies[n].wait_send()
    for j in range(1, NZ):
        hz_copies[j].wait_recv()
    total = hz[0].astype(F32)
    for j in range(1, NZ):
        total = total + hz[j].astype(F32)
    hb[core, me_plane] = total.astype(BF16)

    ha_copies = [None] + [
        remote(hb.at[core, me_plane], hb.at[core, me_plane], ha_s.at[n], ha_r.at[n], plane_at(n)) for n in range(1, PLANE)]
    for n in by_distance[:0:-1]:
        ha_copies[n].start()
    hf_copies = []
    for n in by_distance:
        source = ((x + NX - n // NY) % NX) * NY + (y + NY - n % NY) % NY
        if n:
            ha_copies[n].wait_recv()
        c = remote(hb.at[core, source], hb.at[core, source], hf_s.at[n], hf_r.at[n], sibling)
        c.start()
        hf_copies.append(c)
    for j in range(1, NZ):
        hz_copies[j].wait_send()
    for n in range(1, PLANE):
        ha_copies[n].wait_send()
    for c in hf_copies:
        c.wait()
    head_out[...] = hb[...].reshape(head_out.shape)


def finish(head_in, embed_in, embed_out, head_out, head_f, out_sem):
    pieces = out_sem.shape[0] - 1
    rows = head_f.shape[0] // pieces
    embed_store = pltpu.make_async_copy(embed_in, embed_out, out_sem.at[pieces])
    embed_store.start()
    stores = []
    for i in range(pieces):
        cut = pl.ds(i * rows, rows)
        head_f[cut] = head_in[cut].astype(F32)
        stores.append(pltpu.make_async_copy(head_f.at[cut], head_out.at[cut], out_sem.at[i]))
        stores[i].start()
    for c in stores:
        c.wait()
    embed_store.wait()


def local(batch_index, chip_features, head_weight, probe_left, probe_right):
    points = batch_index.shape[0]
    half = points // 2
    chips, width = chip_features.shape
    probes = probe_left.shape[1]
    embed = head_weight.shape[1]
    rows = width // 2 // PLANE
    norm = 1.0 / math.sqrt(points * PLANE * NZ)
    block = (half, embed)
    vmem, dma = pltpu.VMEM, pltpu.SemaphoreType.DMA
    head, grad = pl.pallas_call(
        functools.partial(fused, norm),
        out_shape=(jax.ShapeDtypeStruct((width, embed), BF16), jax.ShapeDtypeStruct((points, embed), F32)),
        in_specs=[pl.BlockSpec(memory_space=pl.ANY)] * 5,
        out_specs=[pl.BlockSpec(memory_space=pltpu.VMEM)] * 2,
        scratch_shapes=[
            vmem((points,), jnp.int32), vmem((probes, points), BF16), vmem((probes, points), BF16),
            vmem((chips, width), BF16), vmem((width, embed), BF16), vmem((chips, embed), BF16),
            vmem((width // 2, points), BF16), vmem((2, 2) + block, BF16), vmem((2,) + block, BF16),
            vmem((2,) + block, BF16), vmem((2 * PLANE,) + block, BF16), vmem((2 * PLANE,) + block, BF16),
            vmem((2 * PLANE, 8, half), F32), vmem((NZ,) + block, BF16), vmem((NZ,) + block, BF16),
            vmem((NZ,) + block, F32), vmem((NZ,) + block, F32), vmem((NZ,) + block, F32),
            vmem((NZ,) + block, BF16), vmem((NZ,) + block, BF16), vmem((2,) + block, F32),
            vmem((PLANE, rows, embed), BF16), vmem((PLANE, rows, embed), BF16),
            vmem((NZ, rows, embed), BF16), vmem((2, PLANE, rows, embed), BF16),
            dma((4,)), dma((4,)), dma((2,)),
            dma((PLANE,)), dma((PLANE,)), dma((PLANE,)), dma((PLANE,)),
            dma((PLANE,)), dma((PLANE,)), dma((PLANE,)), dma((PLANE,)),
            dma((NZ,)), dma((NZ,)), dma((NZ,)), dma((NZ,)), dma((NZ,)), dma((NZ,)), dma((2,)),
            dma((PLANE,)), dma((PLANE,)), dma((NZ,)), dma((NZ,)),
            dma((PLANE,)), dma((PLANE,)), dma((PLANE,)), dma((PLANE,)),
        ],
        compiler_params=pltpu.CompilerParams(
            collective_id=0, has_side_effects=True, vmem_limit_bytes=48 * 2**20),
    )(*(pltpu.with_memory_space_constraint(a, pltpu.HBM)
        for a in (batch_index, chip_features, head_weight, probe_left.T, probe_right.T)))
    return pl.pallas_call(
        finish,
        out_shape=(jax.ShapeDtypeStruct((points, embed), F32), jax.ShapeDtypeStruct((width, embed), F32)),
        in_specs=[pl.BlockSpec(memory_space=pltpu.VMEM)] * 2,
        out_specs=[pl.BlockSpec(memory_space=pl.ANY)] * 2,
        scratch_shapes=[vmem((width, embed), F32), dma((5,))],
        compiler_params=pltpu.CompilerParams(vmem_limit_bytes=4 * 2**20),
    )(head, grad)


def solution(mesh):
    return jax.shard_map(
        local,
        mesh=mesh,
        in_specs=(P(("row", "col")), P(("row", "col"), None), P(), P(("row", "col"), "cores"), P(("row", "col"), "cores")),
        out_specs=(P(("row", "col"), None), P()),
        check_vma=False,
    )
```

```python
import functools
import math

import jax
import jax.numpy as jnp
from jax import lax
from jax.experimental import pallas as pl
from jax.experimental.pallas import tpu as pltpu
from jax.sharding import PartitionSpec as P

MESH = pl.DeviceIdType.MESH
F32, BF16 = jnp.float32, jnp.bfloat16
NX, NY, NZ = 4, 4, 8
PLANE = NX * NY


def dot(a, b, ca, cb):
    return lax.dot_general(a, b, (((ca,), (cb,)), ((), ())), preferred_element_type=F32)


def squares(z):
    zf = z.astype(F32)
    sq = zf * zf
    hi = sq.astype(BF16)
    return hi, (sq - hi.astype(F32)).astype(BF16)


def fused(norm, idx_hbm, feat_hbm, w_hbm, left_hbm, right_hbm, head_out, embed_out,
          idx_ref, left_ref, right_ref, feat, w, e_all, ft, u_buf, u_in, z_own, zA, lrA, qA, zB, rlB, qB, acc, mass,
          gs, gr, gfull, hp, hr, hz, hb,
          feat_sem, in_sem, u_sem, az_s, az_r, al_s, al_r, fz_s, fz_r, fl_s, fl_r,
          bz_s, bz_r, bl_s, bl_r, g_s, g_r, gx_sem, hr_s, hr_r, hz_s, hz_r, ha_s, ha_r, hf_s, hf_r):
    row, col, core = lax.axis_index("row"), lax.axis_index("col"), lax.axis_index("cores")
    x, y, z = (row // NZ) * 2 + col // NY, col % NY, row % NZ
    half = z_own.shape[1]
    embed = z_own.shape[2]
    scale = 0.5 / embed * math.log2(math.e)

    def at(dx, dy, dz, dc):
        nx, ny, nz = (x + dx) % NX, (y + dy) % NY, (z + dz) % NZ
        return ((nx // 2) * NZ + nz, (nx % 2) * NY + ny, (core + dc) % 2)

    def plane_at(n):
        return at(n // NY, n % NY, 0, 0)

    def remote(src, dst, ssem, rsem, device):
        return pltpu.make_async_remote_copy(
            src_ref=src, dst_ref=dst, send_sem=ssem, recv_sem=rsem, device_id=device, device_id_type=MESH)

    sibling = at(0, 0, 0, 1)
    me_plane = x * NY + y
    other = 1 - core

    near = (1, 3, 2)
    axes = [0] + [NY * d for d in near] + list(near)
    diagonal = [NY * d + e for d in near for e in near]
    order = axes + [PLANE + n for n in axes] + diagonal + [PLANE + n for n in diagonal]
    own = [order.index(n) for n in range(PLANE)]
    passed = [order.index(PLANE + n) for n in range(PLANE)]
    line = [(j + NZ // 2) % NZ for j in range(NZ)]
    early = 2 * len(axes)

    chunk = feat.shape[0] // 4
    small_copies = [
        pltpu.make_async_copy(src, dst, in_sem.at[i])
        for i, (src, dst) in enumerate(((left_hbm, left_ref), (right_hbm, right_ref), (idx_hbm, idx_ref), (w_hbm, w)))]
    for c in small_copies:
        c.start()
    feat_copies = [
        pltpu.make_async_copy(feat_hbm.at[pl.ds(i * chunk, chunk)], feat.at[pl.ds(i * chunk, chunk)], feat_sem.at[i])
        for i in range(4)]
    for c in feat_copies:
        c.start()

    barrier = pltpu.get_barrier_semaphore()
    for n in range(1, PLANE):
        pl.semaphore_signal(barrier, inc=1, device_id=plane_at(n), device_id_type=MESH)
    for j in range(1, NZ):
        pl.semaphore_signal(barrier, inc=1, device_id=at(0, 0, j, 0), device_id_type=MESH)
    pl.semaphore_signal(barrier, inc=1, device_id=sibling, device_id_type=MESH)

    probes = left_ref.shape[0]
    lane = lax.broadcasted_iota(jnp.int32, (probes, embed), 1)
    sub = lax.broadcasted_iota(jnp.int32, (probes, embed), 0)
    first = (lane == sub + 2 * probes * core).astype(F32).astype(BF16)
    second = (lane == sub + 2 * probes * core + probes).astype(F32).astype(BF16)
    small_copies[0].wait()
    small_copies[1].wait()
    lv, rv = left_ref[...], right_ref[...]
    u = (dot(lv, first, 0, 0) + dot(rv, second, 0, 0)).astype(BF16)
    v = (dot(lv, second, 0, 0) + dot(rv, first, 0, 0)).astype(BF16)
    for h in range(2):
        u_buf[h, 0] = u[h * half:(h + 1) * half]
        u_buf[h, 1] = v[h * half:(h + 1) * half]

    small_copies[3].wait()
    for i, c in enumerate(feat_copies):
        c.wait()
        e_all[pl.ds(i * chunk, chunk)] = dot(feat[pl.ds(i * chunk, chunk)], w[...], 1, 0).astype(BF16)

    pl.semaphore_wait(barrier, PLANE - 1 + NZ - 1 + 1)

    sends = []

    def send(src, dst, ssem, rsem, device):
        c = remote(src, dst, ssem, rsem, device)
        c.start()
        sends.append(c)
        return c

    u_copy = send(u_buf.at[other], u_in, u_sem.at[0], u_sem.at[1], sibling)

    small_copies[2].wait()
    index = idx_ref[...].reshape(1, 2 * half)
    onehot = (lax.broadcasted_iota(jnp.int32, (feat.shape[0], 2 * half), 0) == index).astype(F32).astype(BF16)
    z_all = dot(onehot, e_all[...], 0, 0).astype(BF16)
    z_own[0] = z_all[:half]
    z_own[1] = z_all[half:]
    mine = z_own[core]
    zA[own[0]] = mine
    zA[passed[0]] = z_own[other]
    zB[line[0]] = mine

    def send_z(n, m):
        return send(zA.at[own[n]], zA.at[own[m]], az_s.at[m], az_r.at[m], plane_at(m - n))

    def send_l(n, m):
        return send(lrA.at[own[n]], lrA.at[own[m]], al_s.at[m], al_r.at[m], plane_at(m - n))

    def line_z(i, j):
        return send(zB.at[line[i]], zB.at[line[j]], bz_s.at[j], bz_r.at[j], at(0, 0, (j - i) % NZ, 0))

    def line_l(i, j):
        return send(rlB.at[line[i]], rlB.at[line[j]], bl_s.at[j], bl_r.at[j], at(0, 0, (j - i) % NZ, 0))

    def arrived(buf, sem):
        remote(buf, buf, sem, sem, sibling).wait_recv()

    for d in near:
        send_z(0, NY * d)
    line_z(0, 2)
    line_z(0, 6)
    for d in near:
        send_z(0, d)
    line_z(0, 1)
    line_z(0, 7)
    u_copy.wait_recv()
    lrA[own[0]] = u_buf[core, 0] + u_in[0]
    rlB[line[0]] = u_buf[core, 1] + u_in[1]
    for d in near:
        send_l(0, d)
    line_l(0, 2)
    line_l(0, 6)
    for d in near:
        send_l(0, NY * d)
    line_l(0, 1)
    line_l(0, 7)

    def forward_z(n):
        return remote(zA.at[own[n]], zA.at[passed[n]], fz_s.at[n], fz_r.at[n], sibling)

    def forward_l(n):
        return remote(lrA.at[own[n]], lrA.at[passed[n]], fl_s.at[n], fl_r.at[n], sibling)

    forward_l(0).start()
    ones = jnp.ones((8, embed), BF16)
    wide = jnp.ones((embed, embed), BF16)

    def norms_a(p, count):
        hi, lo = squares(zA[p:p + count].reshape(count * half, embed))
        q = (dot(ones, hi, 1, 1) + dot(ones, lo, 1, 1)) * scale
        for i in range(count):
            qA[p + i] = q[:, i * half:(i + 1) * half]

    def norms_b(p, count):
        hi, lo = squares(zB[p:p + count].reshape(count * half, embed))
        qB[p:p + count] = ((dot(hi, wide, 1, 0) + dot(lo, wide, 1, 0)) * scale).reshape(count, half, embed)

    for d in near:
        arrived(zA.at[own[NY * d]], az_r.at[NY * d])
        for e in near:
            send_z(NY * d, NY * d + e)
        forward_z(NY * d).start()
    arrived(zB.at[line[2]], bz_r.at[2])
    line_z(2, 3)
    line_z(2, 4)
    arrived(zB.at[line[6]], bz_r.at[6])
    line_z(6, 5)
    for d in near:
        arrived(lrA.at[own[d]], al_r.at[d])
        for e in near:
            send_l(d, NY * e + d)
        forward_l(d).start()
    arrived(rlB.at[line[2]], bl_r.at[2])
    line_l(2, 3)
    arrived(rlB.at[line[6]], bl_r.at[6])
    line_l(6, 5)
    line_l(6, 4)
    for d in near:
        arrived(zA.at[own[d]], az_r.at[d])
        forward_z(d).start()
        arrived(lrA.at[own[NY * d]], al_r.at[NY * d])
        forward_l(NY * d).start()
    for j in (1, 7):
        arrived(zB.at[line[j]], bz_r.at[j])
        arrived(rlB.at[line[j]], bl_r.at[j])

    def tile(p, count, s, blocks, first):
        rows = blocks * half
        zb = zB[s:s + blocks].reshape(rows, embed)
        rl = rlB[s:s + blocks].reshape(rows, embed)
        qb = qB[s:s + blocks].reshape(rows, embed)
        za = zA[p:p + count].reshape(count * half, embed)
        lr = lrA[p:p + count].reshape(count * half, embed)
        qa = jnp.concatenate([qA[p + i, 0:1] for i in range(count)], axis=1)
        products = dot(zb, za, 1, 1)
        pairs = dot(rl, lr, 1, 1)
        weight = jnp.exp2(products * (2.0 * scale) - (jnp.concatenate([qb] * count, axis=1) + qa)) * pairs
        part = dot(weight.astype(BF16), za, 1, 0).reshape(blocks, half, embed)
        row_mass = weight[:, :half]
        for i in range(1, count):
            row_mass = row_mass + weight[:, i * half:(i + 1) * half]
        row_mass = row_mass.reshape(blocks, half, embed)
        if first:
            acc[s:s + blocks] = part
            mass[s:s + blocks] = row_mass
        else:
            acc[s:s + blocks] += part
            mass[s:s + blocks] += row_mass

    norms_b(line[6], 5)
    norms_a(0, len(axes))
    for n in axes:
        if n:
            arrived(zA.at[passed[n]], fz_r.at[n])
        arrived(lrA.at[passed[n]], fl_r.at[n])
    norms_a(len(axes), len(axes))
    tile(0, early, line[6], 5, True)

    columns = feat.shape[1] // 2
    mine_t = feat[:, pl.ds(pl.multiple_of(core * columns, columns), columns)]
    ft[...] = dot(mine_t, onehot, 0, 0).astype(BF16)


    for n in diagonal:
        arrived(zA.at[own[n]], az_r.at[n])
        forward_z(n).start()
        arrived(lrA.at[own[n]], al_r.at[n])
        forward_l(n).start()
    norms_a(early, len(diagonal))
    for j in (3, 5, 4):
        arrived(zB.at[line[j]], bz_r.at[j])
        arrived(rlB.at[line[j]], bl_r.at[j])
    norms_b(line[4], 2)
    norms_b(line[3], 1)
    tile(0, early, line[4], 2, True)
    for n in diagonal:
        arrived(zA.at[passed[n]], fz_r.at[n])
        arrived(lrA.at[passed[n]], fl_r.at[n])
    norms_a(early + len(diagonal), len(diagonal))

    g_copies = [None] + [remote(gs.at[j], gr.at[j], g_s.at[j], g_r.at[j], at(0, 0, NZ - j, 0)) for j in range(1, NZ)]
    for j in (4, 2, 6, 0):
        s = line[j]
        if j == 2:
            tile(0, early, line[3], 1, True)
        tile(early, 2 * len(diagonal), s, 2, False)
        for i in (1, 0):
            total = jnp.sum(mass[s + i], axis=1, keepdims=True)
            grad = (acc[s + i] - total * zB[s + i].astype(F32)) * (1.0 / embed)
            if j + i == 0:
                acc[s] = grad
            else:
                gs[j + i] = grad.astype(BF16)
                g_copies[j + i].start()

    grad = acc[line[0]]
    for j in range(1, NZ):
        g_copies[j].wait_recv()
        grad = grad + gr[j].astype(F32)
    gfull[core] = grad
    gx = remote(gfull.at[core], gfull.at[core], gx_sem.at[0], gx_sem.at[1], sibling)
    gx.start()

    def head_product(which, value):
        hi = value.astype(BF16)
        lo = (value - hi.astype(F32)).astype(BF16)
        lanes = pl.ds(pl.multiple_of(which * half, half), half)
        return dot(ft[:, lanes], jnp.concatenate([hi, lo], axis=1), 1, 0)

    mine = head_product(core, grad)
    for j in range(1, NZ):
        g_copies[j].wait_send()
    gx.wait()
    product = mine + head_product(other, gfull[other])
    hp[...] = (product[:, :embed] + product[:, embed:]).astype(BF16).reshape(hp.shape)

    def slice_of(n):
        return ((x + n // NY) % NX) * NY + (y + n % NY) % NY

    hr_copies = [None] + [remote(hp.at[slice_of(n)], hr.at[n], hr_s.at[n], hr_r.at[n], plane_at(n)) for n in range(1, PLANE)]
    by_distance = sorted(range(PLANE), key=lambda n: min(n // NY, NX - n // NY) + min(n % NY, NY - n % NY))
    for n in by_distance[:0:-1]:
        hr_copies[n].start()
    embed_out[...] = gfull[...].reshape(2 * half, embed)

    for c in sends:
        c.wait_send()
    for n in range(PLANE):
        if n:
            forward_z(n).wait_send()
        forward_l(n).wait_send()

    total = hp[me_plane].astype(F32)
    for n in by_distance[1:]:
        hr_copies[n].wait_recv()
        total = total + hr[n].astype(F32)
    hz[z] = (total * norm).astype(BF16)

    hz_copies = [None] + [remote(hz.at[z], hz.at[z], hz_s.at[j], hz_r.at[j], at(0, 0, j, 0)) for j in range(1, NZ)]
    for j in (4, 3, 5, 2, 6, 1, 7):
        hz_copies[j].start()
    for n in range(1, PLANE):
        hr_copies[n].wait_send()
    for j in range(1, NZ):
        hz_copies[j].wait_recv()
    total = hz[0].astype(F32)
    for j in range(1, NZ):
        total = total + hz[j].astype(F32)
    hb[core, me_plane] = total.astype(BF16)

    ha_copies = [None] + [
        remote(hb.at[core, me_plane], hb.at[core, me_plane], ha_s.at[n], ha_r.at[n], plane_at(n)) for n in range(1, PLANE)]
    for n in by_distance[:0:-1]:
        ha_copies[n].start()
    hf_copies = []
    for n in by_distance:
        source = ((x + NX - n // NY) % NX) * NY + (y + NY - n % NY) % NY
        if n:
            ha_copies[n].wait_recv()
        c = remote(hb.at[core, source], hb.at[core, source], hf_s.at[n], hf_r.at[n], sibling)
        c.start()
        hf_copies.append(c)
    for j in range(1, NZ):
        hz_copies[j].wait_send()
    for n in range(1, PLANE):
        ha_copies[n].wait_send()
    for c in hf_copies:
        c.wait()
    head_out[...] = hb[...].reshape(head_out.shape)


def finish(head_in, embed_in, embed_out, head_out, head_f, out_sem):
    pieces = out_sem.shape[0] - 1
    rows = head_f.shape[0] // pieces
    embed_store = pltpu.make_async_copy(embed_in, embed_out, out_sem.at[pieces])
    embed_store.start()
    stores = []
    for i in range(pieces):
        cut = pl.ds(i * rows, rows)
        head_f[cut] = head_in[cut].astype(F32)
        stores.append(pltpu.make_async_copy(head_f.at[cut], head_out.at[cut], out_sem.at[i]))
        stores[i].start()
    for c in stores:
        c.wait()
    embed_store.wait()


def local(batch_index, chip_features, head_weight, probe_left, probe_right):
    points = batch_index.shape[0]
    half = points // 2
    chips, width = chip_features.shape
    probes = probe_left.shape[1]
    embed = head_weight.shape[1]
    rows = width // 2 // PLANE
    norm = 1.0 / math.sqrt(points * PLANE * NZ)
    block = (half, embed)
    vmem, dma = pltpu.VMEM, pltpu.SemaphoreType.DMA
    head, grad = pl.pallas_call(
        functools.partial(fused, norm),
        out_shape=(jax.ShapeDtypeStruct((width, embed), BF16), jax.ShapeDtypeStruct((points, embed), F32)),
        in_specs=[pl.BlockSpec(memory_space=pl.ANY)] * 5,
        out_specs=[pl.BlockSpec(memory_space=pltpu.VMEM)] * 2,
        scratch_shapes=[
            vmem((points,), jnp.int32), vmem((probes, points), BF16), vmem((probes, points), BF16),
            vmem((chips, width), BF16), vmem((width, embed), BF16), vmem((chips, embed), BF16),
            vmem((width // 2, points), BF16), vmem((2, 2) + block, BF16), vmem((2,) + block, BF16),
            vmem((2,) + block, BF16), vmem((2 * PLANE,) + block, BF16), vmem((2 * PLANE,) + block, BF16),
            vmem((2 * PLANE, 8, half), F32), vmem((NZ,) + block, BF16), vmem((NZ,) + block, BF16),
            vmem((NZ,) + block, F32), vmem((NZ,) + block, F32), vmem((NZ,) + block, F32),
            vmem((NZ,) + block, BF16), vmem((NZ,) + block, BF16), vmem((2,) + block, F32),
            vmem((PLANE, rows, embed), BF16), vmem((PLANE, rows, embed), BF16),
            vmem((NZ, rows, embed), BF16), vmem((2, PLANE, rows, embed), BF16),
            dma((4,)), dma((4,)), dma((2,)),
            dma((PLANE,)), dma((PLANE,)), dma((PLANE,)), dma((PLANE,)),
            dma((PLANE,)), dma((PLANE,)), dma((PLANE,)), dma((PLANE,)),
            dma((NZ,)), dma((NZ,)), dma((NZ,)), dma((NZ,)), dma((NZ,)), dma((NZ,)), dma((2,)),
            dma((PLANE,)), dma((PLANE,)), dma((NZ,)), dma((NZ,)),
            dma((PLANE,)), dma((PLANE,)), dma((PLANE,)), dma((PLANE,)),
        ],
        compiler_params=pltpu.CompilerParams(
            collective_id=0, has_side_effects=True, vmem_limit_bytes=48 * 2**20),
    )(*(pltpu.with_memory_space_constraint(a, pltpu.HBM)
        for a in (batch_index, chip_features, head_weight, probe_left.T, probe_right.T)))
    return pl.pallas_call(
        finish,
        out_shape=(jax.ShapeDtypeStruct((points, embed), F32), jax.ShapeDtypeStruct((width, embed), F32)),
        in_specs=[pl.BlockSpec(memory_space=pltpu.VMEM)] * 2,
        out_specs=[pl.BlockSpec(memory_space=pl.ANY)] * 2,
        scratch_shapes=[vmem((width, embed), F32), dma((5,))],
        compiler_params=pltpu.CompilerParams(vmem_limit_bytes=4 * 2**20),
    )(head, grad)


def solution(mesh):
    return jax.shard_map(
        local,
        mesh=mesh,
        in_specs=(P(("row", "col")), P(("row", "col"), None), P(), P(("row", "col"), "cores"), P(("row", "col"), "cores")),
        out_specs=(P(("row", "col"), None), P()),
        check_vma=False,
    )
```
